512 devices in a mesh: section: 32 (over x, y), tensor: 16 (over z, core).
Axes of the slice: x: 4, y: 8, z: 8, core: 2. Of those that a mesh axis runs over, the one named last changes fastest.
Arguments:
- frozen: bfloat16 [32, 14336, 2048], P('section', 'tensor'), may hold values from -1 to 1, as said below
- adapter_a: bfloat16 [32, 8, 14336], P('section', None, 'tensor'), may hold values from -0.119628906 to 0.119628906
- adapter_b: bfloat16 [32, 16, 2048], P('section'), may hold values from -0.22460938 to 0.22460938
- magnitude: float32 [32, 2048], P('section'), may hold values from 0.5 to 2
- hidden_fwd: bfloat16 [32, 128, 14336], P('section', None, 'tensor'), may hold values from -6 to 6
- carried: bfloat16 [32, 256, 2048], P('section', 'tensor'), may hold values from -6 to 6
- embedded: bfloat16 [256, 4096], P('tensor'), may hold values from -6 to 6
- hidden_bwd: bfloat16 [32, 128, 14336], P('section', None, 'tensor'), may hold values from -6 to 6
- returned: bfloat16 [32, 256, 2048], P('section', 'tensor'), may hold values from -1.5 to 1.5
- head_grad: bfloat16 [256, 4096], P('tensor'), may hold values from -1.5 to 1.5
Outputs:
- section_out: bfloat16 [32, 256, 2048], P('section', 'tensor')
- grad_magnitude: float32 [32, 2048], P('section')
- grad_a: float32 [32, 8, 14336], P('section', None, 'tensor')
- grad_b: float32 [32, 16, 2048], P('section')
- hidden_grad: bfloat16 [32, 128, 14336], P('section', None, 'tensor')
The draws below stay inside these ranges and needn't reach their ends.
Inputs may be any that keep to these rules, and one draw needn't show every extreme that they name: frozen projection weights.
All inputs are finite; a program needn't handle non-finite values.
Results may differ from the reference program's by a relative error of at most 0.0057.
Values may be sent and summed in bfloat16 or wider, within the bound.
A program may use at most 64 MiB of HBM per device.

```python
import math
import jax
import jax.numpy as jnp
from jax import lax

D = 4096
FF = 14336
R = 16
T_SIZE = 256
SECTIONS = 16
SLOTS = 32


def draw_frozen(key, part):

    def one_slot(slot_num):
        slot_key = jax.random.fold_in(jax.random.fold_in(key, 7001), slot_num)
        key_base, key_rows, key_cols = jax.random.split(slot_key, 3)
        base = jax.random.normal(key_base, (FF, D // 2), jnp.float32)
        slope = 0.55
        row_gain = jnp.exp(jax.random.uniform(key_rows, (FF, 1), jnp.float32, minval=-1.15, maxval=1.15))
        col_gain = jnp.exp(jax.random.uniform(key_cols, (1, D // 2), jnp.float32, minval=-1.15, maxval=1.15))
        trend = jnp.exp(slope * jnp.arange(FF, dtype=jnp.float32) / FF)[:, None]
        row_total = row_gain * trend
        normal_by = jnp.sqrt(jnp.sum(row_total * row_total))
        values = jnp.clip(base * row_total * col_gain / normal_by, -1.0, 1.0)
        return values.astype(jnp.bfloat16)
    return lax.map(one_slot, jnp.arange(SLOTS))


def block_scale(own_key, dims, cuts, low, largest):
    level = 1.0
    for position, shards_of in cuts:
        draws = jax.random.uniform(jax.random.fold_in(jax.random.fold_in(own_key, 6), position), (shards_of,), jnp.float32, low / len(cuts), largest / len(cuts))
        level = level * jnp.repeat(jnp.exp(draws), dims[position] // shards_of).reshape((-1,) + (1,) * (len(dims) - 1 - position))
    return level


def centred(rng, shape, spread, most, shards=(), held_as=jnp.bfloat16):
    result = jax.random.normal(rng, shape, jnp.float32) * spread
    if len(shards) > 0:
        result = block_scale(rng, shape, shards, -0.22, 0.18) * result
    return jnp.clip(result, min=-most, max=most).astype(held_as)


def setup_inputs(seed: int = 0) -> dict:
    key_list = jax.random.split(jax.random.key(seed), 11)
    return {
        "frozen": draw_frozen(jax.random.fold_in(key_list[10], 71), 0),
        "adapter_a": centred(key_list[1], (SLOTS, R // 2, FF), 0.02, 0.119628906, ((0, 32), (2, 16))),
        "adapter_b": centred(key_list[2], (SLOTS, R, D // 2), 0.0375, 0.22460938, ((0, 32),)),
        "magnitude": jnp.clip(jnp.exp(math.log(2.0) - 1.3862944 * jax.random.uniform(key_list[3], (SLOTS, D // 2), jnp.float32) ** block_scale(key_list[3], (SLOTS, D // 2), ((0, 32),), -0.2, 0.2)), 0.5, 2.0),
        "hidden_fwd": centred(key_list[4], (SLOTS, T_SIZE // 2, FF), 1.0, 6.0, ((0, 32), (2, 16))),
        "carried": centred(key_list[5], (SLOTS, T_SIZE, D // 2), 1.0, 6.0, ((0, 32), (1, 16))),
        "embedded": centred(key_list[6], (T_SIZE, D), 1.0, 6.0, ((0, 16),)),
        "hidden_bwd": centred(key_list[7], (SLOTS, T_SIZE // 2, FF), 1.0, 6.0, ((0, 32), (2, 16))),
        "returned": centred(key_list[8], (SLOTS, T_SIZE, D // 2), 0.25, 1.5, ((0, 32), (1, 16))),
        "head_grad": centred(key_list[9], (T_SIZE, D), 0.25, 1.5, ((0, 16),)),
    }


epsilon = 1e-06

def one_section(packed):
    base_pair, fac_a, fac_pair, mag, hid_fwd, inflow, hid_bwd, cot = packed
    base_w = jnp.concatenate([base_pair[0], base_pair[1]], axis=1)
    fac_b = jnp.concatenate([fac_pair[0], fac_pair[1]], axis=1)
    merged = (base_w.astype(jnp.float32) + jnp.dot(fac_a.T, fac_b, preferred_element_type=jnp.float32)).astype(jnp.bfloat16)
    merged_f = merged.astype(jnp.float32)
    col_norms = jnp.sqrt(lax.optimization_barrier(jnp.sum(merged_f * merged_f, axis=0)) + epsilon)
    col_scale = mag / col_norms
    projected = jnp.dot(hid_fwd, merged, preferred_element_type=jnp.float32)
    section_out = (inflow.astype(jnp.float32) + projected * col_scale).astype(jnp.bfloat16)
    low = jnp.dot(hid_bwd, fac_a.T, preferred_element_type=jnp.float32).astype(jnp.bfloat16)
    recomputed = jnp.dot(hid_bwd, merged, preferred_element_type=jnp.float32)
    grad_mag = lax.optimization_barrier(jnp.sum(cot.astype(jnp.float32) * recomputed, axis=0)) / col_norms
    scaled_cot = (cot.astype(jnp.float32) * col_scale).astype(jnp.bfloat16)
    hidden_grad = jnp.dot(scaled_cot, merged.T, preferred_element_type=jnp.float32).astype(jnp.bfloat16)
    adapter_cot = jnp.dot(scaled_cot, fac_b.T, preferred_element_type=jnp.float32).astype(jnp.bfloat16)
    grad_a = jnp.dot(adapter_cot.T, hid_bwd, preferred_element_type=jnp.float32)
    grad_b = jnp.dot(low.T, scaled_cot, preferred_element_type=jnp.float32)
    return (section_out, grad_mag, grad_a, grad_b, hidden_grad)

def join_cols(values):
    paired = values.reshape((SECTIONS, 2) + values.shape[1:])
    return jnp.concatenate([paired[:, 0], paired[:, 1]], axis=-1)

def split_cols(values):
    half = values.shape[-1] // 2
    stacked = jnp.stack([values[..., :half], values[..., half:]], axis=1)
    return stacked.reshape((SECTIONS * 2,) + values.shape[1:-1] + (half,))

def reference(frozen, adapter_a, adapter_b, magnitude, hidden_fwd, carried, embedded, hidden_bwd, returned, head_grad):
    base_pairs = frozen.reshape((SECTIONS, 2) + frozen.shape[1:])
    fac_pairs = adapter_b.reshape((SECTIONS, 2) + adapter_b.shape[1:])
    fac_a = adapter_a.reshape((SECTIONS, R, FF))
    mag = magnitude.reshape((SECTIONS, D))
    hid_fwd = hidden_fwd.reshape((SECTIONS, T_SIZE, FF))
    hid_bwd = hidden_bwd.reshape((SECTIONS, T_SIZE, FF))
    carried_full = join_cols(carried)
    returned_full = join_cols(returned)
    inflow = jnp.concatenate([embedded[None], carried_full[:-1]], axis=0)
    cot = jnp.concatenate([returned_full[1:], head_grad[None]], axis=0)
    section_out, grad_mag, grad_a, grad_b, hidden_grad = lax.map(one_section, (base_pairs, fac_a, fac_pairs, mag, hid_fwd, inflow, hid_bwd, cot))
    return (split_cols(section_out), grad_mag.reshape((SECTIONS * 2, D // 2)), grad_a.reshape((SECTIONS * 2, R // 2, FF)), split_cols(grad_b), hidden_grad.reshape((SECTIONS * 2, T_SIZE // 2, FF)))
```

```python
import jax
import jax.numpy as jnp
from jax import lax
from jax.experimental import pallas as pl
from jax.experimental.pallas import tpu as pltpu
from jax.sharding import PartitionSpec as P

epsilon = 1e-06
bf16 = jnp.bfloat16
f32 = jnp.float32


def dot(left, right, left_dim, right_dim):
    return lax.dot_general(
        left, right, (((left_dim,), (right_dim,)), ((), ())), preferred_element_type=f32
    )


def make_kernel(secs, tens, names, n_sems):
    rings = tens // 2
    far = rings // 2

    def kernel(*refs):
        (w_in, a_in, b_in, mag_in, hf_in, car_in, emb_in, hb_in, ret_in, head_in) = refs[:10]
        (so_out, gm_out, ga_out, gb_out, hg_out) = refs[10:15]
        s = dict(zip(names, refs[15:]))
        w, a_own, a_oth, b, mag = s["w"], s["a_own"], s["a_oth"], s["b"], s["mag"]
        xf, xb, infl, cot, scot = s["xf"], s["xb"], s["infl"], s["cot"], s["scot"]
        sems = s["sems"]
        used = [0]

        def sem():
            used[0] += 1
            assert used[0] <= n_sems
            return sems.at[used[0] - 1]

        depth, width = w.shape
        wide = width // 2
        half_rows = xb.shape[1]
        blocks = half_rows // 16

        sec = lax.axis_index("section")
        ten = lax.axis_index("tensor")
        half = lax.rem(sec, 2)
        core = lax.rem(ten, 2)
        z = ten // 2
        partner = {"section": sec + 1 - 2 * half}
        sibling = {"tensor": ten + 1 - 2 * core}
        next_sec = {"section": lax.rem(sec + 2, secs)}
        prev_sec = {"section": lax.rem(sec + secs - 2, secs)}
        up = {"tensor": lax.rem(ten + 2, tens)}
        down = {"tensor": lax.rem(ten + tens - 2, tens)}

        def remote(src, dst, where):
            return pltpu.make_async_remote_copy(
                src_ref=src,
                dst_ref=dst,
                send_sem=sem(),
                recv_sem=sem(),
                device_id=where,
                device_id_type=pl.DeviceIdType.MESH,
            )

        def local(src, dst):
            return pltpu.make_async_copy(src, dst, sem())

        def cols(q):
            return pl.ds(q * wide, wide)

        sent = []

        def start(*copies):
            for copy in copies:
                copy.start()
                sent.append(copy)

        ld_a = local(a_in.at[0], a_own)
        ld_b = local(b_in.at[0], b)
        ld_w = local(w_in.at[0], w)
        ld_mag = local(mag_in, mag)
        ld_hb = local(hb_in.at[0], xb.at[half])
        ld_hf = [local(hf_in.at[:, p], xf.at[p, pl.ds(half * (blocks // 2), blocks // 2)]) for p in (0, 1)]
        own_cols = pl.ds(pl.multiple_of(half * width, 128), width)
        ld_infl = local(emb_in.at[:, own_cols], infl)
        ld_cot = local(head_in.at[:, own_cols], cot.at[ten])
        for copy in (ld_a, ld_b, ld_w, ld_hb, ld_mag, *ld_hf):
            copy.start()

        @pl.when(sec < 2)
        def _():
            ld_infl.start()

        @pl.when(sec >= secs - 2)
        def _():
            ld_cot.start()

        barrier = pltpu.get_barrier_semaphore()
        peers = [{"tensor": lax.rem(ten + k, tens)} for k in range(1, tens)]
        everyone = [partner, next_sec, prev_sec] + peers
        for where in everyone:
            pl.semaphore_signal(barrier, inc=1, device_id=where, device_id_type=pl.DeviceIdType.MESH)
        pl.semaphore_wait(barrier, len(everyone))

        sw_a = remote(a_in.at[0], a_oth, partner)
        sw_ret = remote(ret_in.at[0], cot.at[ten], prev_sec)
        sw_hf = [
            remote(hf_in.at[:, p], xf.at[p, pl.ds(half * (blocks // 2), blocks // 2)], partner)
            for p in (0, 1)
        ]
        sw_hb = remote(hb_in.at[0], xb.at[half], partner)
        sw_car = remote(car_in.at[0], infl, next_sec)
        start(sw_a)

        @pl.when(sec >= 2)
        def _():
            sw_ret.start()

        start(*sw_hf, sw_hb)

        @pl.when(sec < secs - 2)
        def _():
            sw_car.start()

        def block(zz):
            return lax.rem(zz + rings, rings) * 2 + core

        def gather_copy(k, q, sign, where):
            ref = cot.at[block(z - sign * (k - 1)), :, cols(q)]
            return remote(ref, ref, where)

        ag_up = {(k, q): gather_copy(k, q, 1, up) for k in range(1, far + 1) for q in (0, 1) if k < far or q == 0}
        ag_dn = {(k, q): gather_copy(k, q, -1, down) for k in range(1, far + 1) for q in (0, 1) if k < far or q == 1}

        def cross(zz, q=None):
            ref = cot.at[block(zz)] if q is None else cot.at[block(zz), :, cols(q)]
            return remote(ref, ref, sibling)

        ag_x = [cross(z)]

        def gather_first():
            @pl.when(sec < secs - 2)
            def _():
                sw_ret.wait_recv()

            @pl.when(sec >= secs - 2)
            def _():
                ld_cot.wait()

            for q in (0, 1):
                for ag in (ag_up, ag_dn):
                    if (1, q) in ag:
                        start(ag[1, q])
            start(ag_x[0])

        def gather_step(k):
            for q in (0, 1):
                for ag in (ag_up, ag_dn):
                    if (k, q) in ag:
                        ag[k, q].wait_recv()
                        if (k + 1, q) in ag:
                            start(ag[k + 1, q])
            if k < far:
                more = [cross(z - k), cross(z + k)]
            else:
                more = [cross(z - k, 0), cross(z + k, 1)]
            start(*more)
            ag_x.extend(more)

        def total_of(part, sib, slots, own_half):
            first = remote(part, sib, sibling)

            def stage1():
                start(first)

            copies = []

            def stage2():
                first.wait_recv()
                slots[z] = part[...] + sib[...]
                ref = slots.at[(z, *own_half)]
                for k in range(1, rings):
                    for other in (0, 1):
                        there = lax.rem(z + k, rings) * 2 + (core if other == 0 else 1 - core)
                        copies.append(remote(ref, ref, {"tensor": there}))
                start(*copies)

            def stage3():
                for copy in copies:
                    copy.wait_recv()
                total = slots[0]
                for k in range(1, rings):
                    total = total + slots[k]
                return total

            return stage1, stage2, stage3

        lane_half = (slice(None), pl.ds(pl.multiple_of(core * wide, 128), wide))
        row_half = (pl.ds(pl.multiple_of(core * 8, 8), 8), slice(None))
        sq1, sq2, sq3 = total_of(s["sq"], s["sq_sib"], s["sq_slots"], lane_half)
        gm1, gm2, gm3 = total_of(s["gmp"], s["gm_sib"], s["gm_slots"], lane_half)
        lo1, lo2, lo3 = total_of(s["lo"], s["lo_sib"], s["lo_slots"], row_half)

        ld_a.wait()
        ld_b.wait()
        ld_hb.wait()
        sw_a.wait_recv()
        mine, theirs = a_own[...].astype(f32), a_oth[...].astype(f32)
        first = half == 0
        a_all = jnp.concatenate(
            [jnp.where(first, mine, theirs), jnp.where(first, theirs, mine)], axis=0
        )
        s["at"][...] = a_all.T.astype(bf16)
        s["lo"][...] = dot(a_all.astype(bf16), xb[half], 1, 1)
        lo1()

        step_cols = min(256, width)
        step_rows = min(128, depth)

        def merge(i, carry):
            cc = pl.ds(pl.multiple_of(i * step_cols, step_cols), step_cols)
            b_c = b[:, cc]
            total = jnp.zeros((8, step_cols), f32)
            for r in range(0, depth, step_rows):
                rr = pl.ds(r, step_rows)
                m = (w[rr, cc].astype(f32) + dot(s["at"][rr, :], b_c, 1, 0)).astype(bf16)
                w[rr, cc] = m
                m = m.astype(f32)
                total = total + jnp.sum((m * m).reshape(step_rows // 8, 8, step_cols), axis=0)
            s["sq"][:, cc] = jnp.sum(total, axis=0, keepdims=True)
            return carry

        ld_w.wait()
        n_merge = width // step_cols
        lax.fori_loop(0, n_merge // 2, merge, 0)
        gather_first()
        lo2()
        lax.fori_loop(n_merge // 2, n_merge, merge, 0)
        sq1()
        gather_step(1)
        sq2()
        low_own = lo3().astype(bf16)
        s["low_own"][...] = low_own
        sw_low = remote(s["low_own"], s["low_oth"], partner)
        start(sw_low)
        if far > 2:
            gather_step(2)

        for copy in ld_hf:
            copy.wait()
        for copy in sw_hf:
            copy.wait_recv()
        pcols = min(512, width)

        def project(parity, keep):
            def body(i, carry):
                cc = pl.ds(pl.multiple_of(i * pcols, pcols), pcols)
                x = xf[parity].reshape(half_rows, depth)
                res = dot(x, w[:, cc], 1, 0)
                keep[:, :, cc] = res.reshape(rings, 16, pcols).astype(keep.dtype)
                return carry

            lax.fori_loop(0, width // pcols, body, 0)

        project(1 - core, s["p_send"])
        sw_p = remote(s["p_send"], s["p_recv"], sibling)
        start(sw_p)
        for k in range(3 if far > 2 else 2, far):
            gather_step(k)
        project(core, s["pm"])
        gather_step(far)

        ld_mag.wait()
        norms = jnp.sqrt(sq3() + epsilon)
        s["norms"][...] = norms
        s["scale"][...] = mag[...] / norms
        for copy in ag_x:
            copy.wait_recv()

        def rescale(i, carry):
            scot[i] = (cot[i].astype(f32) * s["scale"][...]).astype(bf16)
            return carry

        lax.fori_loop(0, tens, rescale, 0)

        hsplit = [(0, depth)] if depth < 896 else [(0, 512), (512, depth - 512)]

        def hidden(which, lo, size):
            rows = scot[pl.ds(which * blocks, blocks)].reshape(half_rows, width)
            return dot(rows, w[pl.ds(lo, size), :], 1, 1)

        sw_hg = []
        for lo, size in hsplit:
            s["hg_send"][:, pl.ds(lo, size)] = hidden(1 - half, lo, size).astype(bf16)
            copy = remote(s["hg_send"].at[:, pl.ds(lo, size)], s["hg_recv"].at[:, pl.ds(lo, size)], partner)
            start(copy)
            sw_hg.append(copy)

        adapt = dot(b[...], scot[...].reshape(2 * half_rows, width), 1, 1)
        s["ad"][...] = adapt.reshape(2, 8, 2 * half_rows)
        sw_ad = remote(s["ad"].at[1 - half], s["ad_recv"], partner)
        start(sw_ad)

        pm = s["pm"]
        sw_p.wait_recv()

        def merge_cores(i, carry):
            pm[i] = pm[i] + s["p_recv"][i].astype(f32)
            return carry

        lax.fori_loop(0, rings, merge_cores, 0)
        rs = {}

        def scatter_step(k):
            for q in (0, 1):
                for name, sign, first_q, where in (("u", 1, 0, up), ("d", -1, 1, down)):
                    if k == 1 and q != first_q:
                        continue
                    dest = lax.rem(z + sign * (far + 1 - k) + rings, rings)
                    val = pm[dest, :, cols(q)]
                    if (name, k - 1, q) in rs:
                        rs[name, k - 1, q].wait_recv()
                        val = val + s["rs_recv_" + name][k - 2, :, cols(q)].astype(f32)
                    s["rs_send_" + name][k - 1, :, cols(q)] = val.astype(bf16)
                    copy = remote(
                        s["rs_send_" + name].at[k - 1, :, cols(q)],
                        s["rs_recv_" + name].at[k - 1, :, cols(q)],
                        where,
                    )
                    start(copy)
                    rs[name, k, q] = copy

        scatter_step(1)

        for i, (lo, size) in enumerate(hsplit):
            s["hg_own"][:, pl.ds(lo, size)] = hidden(half, lo, size)
        scatter_step(2)

        sw_hb.wait_recv()

        def recompute(i, carry):
            cc = pl.ds(pl.multiple_of(i * step_cols, step_cols), step_cols)
            res = dot(xb[...].reshape(2 * half_rows, depth), w[:, cc], 1, 0)
            got = cot[:, :, cc].reshape(2 * half_rows, step_cols).astype(f32)
            part = jnp.sum((res * got).reshape(half_rows // 4, 8, step_cols), axis=0)
            s["gmp"][:, cc] = jnp.sum(part, axis=0, keepdims=True)
            return carry

        n_rec = width // step_cols
        lax.fori_loop(0, n_rec // 2, recompute, 0)
        if far > 2:
            scatter_step(3)
        lax.fori_loop(n_rec // 2, n_rec, recompute, 0)
        gm1()
        for k in range(4 if far > 2 else 3, far + 1):
            scatter_step(k)
        gm2()

        sw_ad.wait_recv()
        own_ad = (s["ad"][half] + s["ad_recv"][...]).astype(bf16)
        s["ga"][...] = dot(own_ad, xb[...].reshape(2 * half_rows, depth), 1, 0)
        out_ga = local(s["ga"], ga_out.at[0])
        out_ga.start()
        sw_low.wait_recv()
        s["gb"][...] = dot(
            s["low_own"][...], scot[pl.ds(half * blocks, blocks)].reshape(half_rows, width), 1, 0
        ) + dot(
            s["low_oth"][...], scot[pl.ds((1 - half) * blocks, blocks)].reshape(half_rows, width), 1, 0
        )
        out_gb = local(s["gb"], gb_out.at[0])
        out_gb.start()

        @pl.when(sec < 2)
        def _():
            ld_infl.wait()

        @pl.when(sec >= 2)
        def _():
            sw_car.wait_recv()

        for q in (0, 1):
            val = pm[z, :, cols(q)]
            for name in "ud":
                if (name, far, q) in rs:
                    rs[name, far, q].wait_recv()
                    val = val + s["rs_recv_" + name][far - 1, :, cols(q)].astype(f32)
            val = infl[:, cols(q)].astype(f32) + val * s["scale"][:, cols(q)]
            s["so"][:, cols(q)] = val.astype(bf16)
        out_so = local(s["so"], so_out.at[0])
        out_so.start()

        s["gm"][...] = gm3() / s["norms"][...]
        out_gm = local(s["gm"], gm_out)
        out_gm.start()

        for copy in sw_hg:
            copy.wait_recv()
        s["hg"][...] = (s["hg_own"][...] + s["hg_recv"][...].astype(f32)).astype(bf16)
        out_hg = local(s["hg"], hg_out.at[0])
        out_hg.start()

        for copy in sent:
            copy.wait_send()

        @pl.when(sec >= 2)
        def _():
            sw_ret.wait_send()

        @pl.when(sec < secs - 2)
        def _():
            sw_car.wait_send()

        for copy in (out_ga, out_gb, out_so, out_gm, out_hg):
            copy.wait()

    return kernel


def local(secs, tens, *args):
    (frozen, adapter_a, adapter_b, magnitude, hidden_fwd, carried, embedded, hidden_bwd, returned, head) = args
    depth, width = frozen.shape[1:]
    half_rows = hidden_fwd.shape[1]
    rings = tens // 2
    far = rings // 2
    n_sems = 320
    shapes = {
        "w": pltpu.VMEM((depth, width), bf16),
        "a_own": pltpu.VMEM((8, depth), bf16),
        "a_oth": pltpu.VMEM((8, depth), bf16),
        "at": pltpu.VMEM((depth, 16), bf16),
        "b": pltpu.VMEM((16, width), bf16),
        "mag": pltpu.VMEM((1, width), f32),
        "norms": pltpu.VMEM((1, width), f32),
        "scale": pltpu.VMEM((1, width), f32),
        "xf": pltpu.VMEM((2, rings, 16, depth), bf16),
        "xb": pltpu.VMEM((2, half_rows, depth), bf16),
        "infl": pltpu.VMEM((16, width), bf16),
        "cot": pltpu.VMEM((tens, 16, width), bf16),
        "scot": pltpu.VMEM((tens, 16, width), bf16),
        "sq": pltpu.VMEM((1, width), f32),
        "sq_sib": pltpu.VMEM((1, width), f32),
        "sq_slots": pltpu.VMEM((rings, 1, width), f32),
        "gmp": pltpu.VMEM((1, width), f32),
        "gm_sib": pltpu.VMEM((1, width), f32),
        "gm_slots": pltpu.VMEM((rings, 1, width), f32),
        "lo": pltpu.VMEM((16, half_rows), f32),
        "lo_sib": pltpu.VMEM((16, half_rows), f32),
        "lo_slots": pltpu.VMEM((rings, 16, half_rows), f32),
        "low_own": pltpu.VMEM((16, half_rows), bf16),
        "low_oth": pltpu.VMEM((16, half_rows), bf16),
        "p_send": pltpu.VMEM((rings, 16, width), bf16),
        "p_recv": pltpu.VMEM((rings, 16, width), bf16),
        "pm": pltpu.VMEM((rings, 16, width), f32),
        "rs_send_u": pltpu.VMEM((far, 16, width), bf16),
        "rs_recv_u": pltpu.VMEM((far, 16, width), bf16),
        "rs_send_d": pltpu.VMEM((far, 16, width), bf16),
        "rs_recv_d": pltpu.VMEM((far, 16, width), bf16),
        "hg_send": pltpu.VMEM((half_rows, depth), bf16),
        "hg_recv": pltpu.VMEM((half_rows, depth), bf16),
        "hg_own": pltpu.VMEM((half_rows, depth), f32),
        "ad": pltpu.VMEM((2, 8, 2 * half_rows), f32),
        "ad_recv": pltpu.VMEM((8, 2 * half_rows), f32),
        "so": pltpu.VMEM((16, width), bf16),
        "gm": pltpu.VMEM((1, width), f32),
        "ga": pltpu.VMEM((8, depth), f32),
        "gb": pltpu.VMEM((16, width), f32),
        "hg": pltpu.VMEM((half_rows, depth), bf16),
        "sems": pltpu.SemaphoreType.DMA((n_sems,)),
    }
    anywhere = pl.BlockSpec(memory_space=pl.ANY)
    return pl.pallas_call(
        make_kernel(secs, tens, list(shapes), n_sems),
        out_shape=(
            jax.ShapeDtypeStruct((1, 16, width), bf16),
            jax.ShapeDtypeStruct((1, width), f32),
            jax.ShapeDtypeStruct((1, 8, depth), f32),
            jax.ShapeDtypeStruct((1, 16, width), f32),
            jax.ShapeDtypeStruct((1, half_rows, depth), bf16),
        ),
        in_specs=[anywhere] * 10,
        out_specs=(anywhere,) * 5,
        scratch_shapes=list(shapes.values()),
        compiler_params=pltpu.CompilerParams(
            collective_id=0, has_side_effects=True, vmem_limit_bytes=48 * 1024 * 1024
        ),
    )(
        frozen,
        adapter_a,
        adapter_b,
        magnitude,
        hidden_fwd.reshape(half_rows // 32, 2, 16, depth),
        carried,
        embedded,
        hidden_bwd,
        returned,
        head,
    )


def solution(mesh):
    secs, tens = mesh.shape["section"], mesh.shape["tensor"]
    placed = (
        P("section", "tensor", None),
        P("section", None, "tensor"),
        P("section", None, None),
        P("section", None),
        P("section", None, "tensor"),
        P("section", "tensor", None),
        P("tensor", None),
        P("section", None, "tensor"),
        P("section", "tensor", None),
        P("tensor", None),
    )

    def run(*args):
        return local(secs, tens, *args)

    return jax.shard_map(
        run,
        mesh=mesh,
        in_specs=placed,
        out_specs=(
            P("section", "tensor", None),
            P("section", None),
            P("section", None, "tensor"),
            P("section", None, None),
            P("section", None, "tensor"),
        ),
        check_vma=False,
    )
```

```python
import jax
import jax.numpy as jnp
from jax import lax
from jax.experimental import pallas as pl
from jax.experimental.pallas import tpu as pltpu
from jax.sharding import PartitionSpec as P

epsilon = 1e-06
bf16 = jnp.bfloat16
f32 = jnp.float32


def dot(left, right, left_dim, right_dim):
    return lax.dot_general(
        left, right, (((left_dim,), (right_dim,)), ((), ())), preferred_element_type=f32
    )


def make_kernel(secs, tens, names, n_sems):
    rings = tens // 2
    assert rings == 8

    def kernel(*refs):
        (w_in, a_in, b_in, mag_in, hf_in, car_in, emb_in, hb_in, ret_in, head_in) = refs[:10]
        (so_out, gm_out, ga_out, gb_out, hg_out) = refs[10:15]
        s = dict(zip(names, refs[15:]))
        w, a_own, a_oth, b, mag = s["w"], s["a_own"], s["a_oth"], s["b"], s["mag"]
        xf, xb, infl, cot, scot = s["xf"], s["xb"], s["infl"], s["cot"], s["scot"]
        sems = s["sems"]
        used = [0]

        def sem():
            used[0] += 1
            assert used[0] <= n_sems
            return sems.at[used[0] - 1]

        depth, width = w.shape
        wide = width // 2
        half_rows = xb.shape[1]
        blocks = half_rows // 16

        sec = lax.axis_index("section")
        ten = lax.axis_index("tensor")
        half = lax.rem(sec, 2)
        core = lax.rem(ten, 2)
        z = ten // 2
        partner = {"section": sec + 1 - 2 * half}
        sibling = {"tensor": ten + 1 - 2 * core}
        next_sec = {"section": lax.rem(sec + 2, secs)}
        prev_sec = {"section": lax.rem(sec + secs - 2, secs)}

        def remote(src, dst, where):
            return pltpu.make_async_remote_copy(
                src_ref=src,
                dst_ref=dst,
                send_sem=sem(),
                recv_sem=sem(),
                device_id=where,
                device_id_type=pl.DeviceIdType.MESH,
            )

        def local(src, dst):
            return pltpu.make_async_copy(src, dst, sem())

        def cols(q):
            return pl.ds(q * wide, wide)

        sent = []

        def start(*copies):
            for copy in copies:
                copy.start()
                sent.append(copy)

        ld_a = local(a_in.at[0], a_own)
        ld_b = local(b_in.at[0], b)
        ld_w = local(w_in.at[0], w)
        ld_mag = local(mag_in, mag)
        ld_hb = local(hb_in.at[0], xb.at[half])
        ld_hf = [local(hf_in.at[:, p], xf.at[p, pl.ds(half * (blocks // 2), blocks // 2)]) for p in (0, 1)]
        own_cols = pl.ds(pl.multiple_of(half * width, 128), width)
        ld_infl = local(emb_in.at[:, own_cols], infl)
        ld_cot = local(head_in.at[:, own_cols], cot.at[ten])
        for copy in (ld_a, ld_b, ld_w, ld_hb, ld_mag, *ld_hf):
            copy.start()

        @pl.when(sec < 2)
        def _():
            ld_infl.start()

        @pl.when(sec >= secs - 2)
        def _():
            ld_cot.start()

        barrier = pltpu.get_barrier_semaphore()
        peers = [{"tensor": lax.rem(ten + k, tens)} for k in range(1, tens)]
        everyone = [partner, next_sec, prev_sec] + peers
        for where in everyone:
            pl.semaphore_signal(barrier, inc=1, device_id=where, device_id_type=pl.DeviceIdType.MESH)
        pl.semaphore_wait(barrier, len(everyone))

        sw_a = remote(a_in.at[0], a_oth, partner)
        sw_ret = remote(ret_in.at[0], cot.at[ten], prev_sec)
        sw_hf = [
            remote(hf_in.at[:, p], xf.at[p, pl.ds(half * (blocks // 2), blocks // 2)], partner)
            for p in (0, 1)
        ]
        sw_hb = remote(hb_in.at[0], xb.at[half], partner)
        sw_car = remote(car_in.at[0], infl, next_sec)
        start(sw_a)

        @pl.when(sec >= 2)
        def _():
            sw_ret.start()

        def at_ring(k):
            return lax.rem(z + k + rings, rings)

        def on_ring(k):
            return {"tensor": at_ring(k) * 2 + core}

        def cot_copy(k, q, where):
            ref = cot.at[at_ring(k) * 2 + core]
            if q is not None:
                ref = cot.at[at_ring(k) * 2 + core, :, cols(q)]
            return remote(ref, ref, where)

        first_q = {1: 0, -1: 1}
        ag_own = {k: cot_copy(0, None, on_ring(k)) for k in (2, -2, 1, -1)}
        ag_far = {}
        ag_x = []

        def cross(k):
            ag_x.append(cot_copy(k, None, sibling))
            start(ag_x[-1])

        def gather_first():
            @pl.when(sec < secs - 2)
            def _():
                sw_ret.wait_recv()

            @pl.when(sec >= secs - 2)
            def _():
                ld_cot.wait()

            start(*ag_own.values())
            cross(0)

        def gather_second():
            for d in (1, -1):
                ag_own[2 * d].wait_recv()
                ag_far[3 * d] = cot_copy(-2 * d, None, on_ring(d))
                ag_far[4 * d] = cot_copy(-2 * d, first_q[d], on_ring(2 * d))
                start(ag_far[3 * d], ag_far[4 * d])
                cross(-2 * d)

        def gather_near():
            for d in (1, -1):
                ag_own[d].wait_recv()
                cross(-d)

        def gather_last():
            for d in (1, -1):
                ag_far[3 * d].wait_recv()
                cross(-3 * d)
            for d in (1, -1):
                ag_far[4 * d].wait_recv()
            cross(4)
            for copy in ag_x:
                copy.wait_recv()

        def total_of(part, sib, slots, own_half):
            first = remote(part, sib, sibling)

            def stage1():
                start(first)

            copies = []

            def stage2():
                first.wait_recv()
                slots[z] = part[...] + sib[...]
                ref = slots.at[(z, *own_half)]
                for k in range(1, rings):
                    for other in (0, 1):
                        there = lax.rem(z + k, rings) * 2 + (core if other == 0 else 1 - core)
                        copies.append(remote(ref, ref, {"tensor": there}))
                start(*copies)

            def stage3():
                for copy in copies:
                    copy.wait_recv()
                total = slots[0]
                for k in range(1, rings):
                    total = total + slots[k]
                return total

            return stage1, stage2, stage3

        lane_half = (slice(None), pl.ds(pl.multiple_of(core * wide, 128), wide))
        row_half = (pl.ds(pl.multiple_of(core * 8, 8), 8), slice(None))
        sq1, sq2, sq3 = total_of(s["sq"], s["sq_sib"], s["sq_slots"], lane_half)
        gm1, gm2, gm3 = total_of(s["gmp"], s["gm_sib"], s["gm_slots"], lane_half)
        lo1, lo2, lo3 = total_of(s["lo"], s["lo_sib"], s["lo_slots"], row_half)

        ld_a.wait()
        ld_b.wait()
        sw_a.wait_recv()
        start(*sw_hf)
        mine, theirs = a_own[...].astype(f32), a_oth[...].astype(f32)
        first = half == 0
        a_all = jnp.concatenate(
            [jnp.where(first, mine, theirs), jnp.where(first, theirs, mine)], axis=0
        )
        s["at"][...] = a_all.T.astype(bf16)

        step_cols = min(256, width)
        step_rows = min(128, depth)

        def merge(i, carry):
            cc = pl.ds(pl.multiple_of(i * step_cols, step_cols), step_cols)
            b_c = b[:, cc]
            total = jnp.zeros((8, step_cols), f32)
            for r in range(0, depth, step_rows):
                rr = pl.ds(r, step_rows)
                m = (w[rr, cc].astype(f32) + dot(s["at"][rr, :], b_c, 1, 0)).astype(bf16)
                w[rr, cc] = m
                m = m.astype(f32)
                total = total + jnp.sum((m * m).reshape(step_rows // 8, 8, step_cols), axis=0)
            s["sq"][:, cc] = jnp.sum(total, axis=0, keepdims=True)
            return carry

        ld_w.wait()
        n_merge = width // step_cols
        lax.fori_loop(0, n_merge * 5 // 8, merge, 0)
        gather_first()
        lax.fori_loop(n_merge * 5 // 8, n_merge, merge, 0)
        sq1()

        ld_hb.wait()
        s["lo"][...] = dot(a_all.astype(bf16), xb[half], 1, 1)
        lo1()
        sq2()

        for copy in ld_hf:
            copy.wait()
        for copy in sw_hf:
            copy.wait_recv()
        start(sw_hb)

        pcols = min(512, width)

        def project(parity, keep, lo, hi):
            def body(i, carry):
                cc = pl.ds(pl.multiple_of(i * pcols, pcols), pcols)
                x = xf[parity].reshape(half_rows, depth)
                res = dot(x, w[:, cc], 1, 0)
                keep[:, :, cc] = res.reshape(rings, 16, pcols).astype(keep.dtype)
                return carry

            lax.fori_loop(lo // pcols, hi // pcols, body, 0)

        sw_p = []
        for q in (0, 1):
            project(1 - core, s["p_send"], q * wide, (q + 1) * wide)
            sw_p.append(remote(s["p_send"].at[:, :, cols(q)], s["p_recv"].at[:, :, cols(q)], sibling))
            start(sw_p[q])
        project(core, s["pm"], 0, width)
        gather_second()
        for copy in sw_p:
            copy.wait_recv()

        pm = s["pm"]

        def term(k, q=None):
            cc = slice(None) if q is None else cols(q)
            return pm[at_ring(k), :, cc] + s["p_recv"][at_ring(k), :, cc].astype(f32)

        rs = {}

        def scatter(name, slot, val, q, where):
            cc = slice(None) if q is None else cols(q)
            s["rs_send"][slot, :, cc] = val.astype(bf16)
            copy = remote(s["rs_send"].at[slot, :, cc], s["rs_recv"].at[slot, :, cc], where)
            start(copy)
            rs[name] = copy

        def landed(name, slot, q=None):
            cc = slice(None) if q is None else cols(q)
            rs[name].wait_recv()
            return s["rs_recv"][slot, :, cc].astype(f32)

        ways = ((0, 1), (1, -1))
        for i, d in ways:
            scatter(("b", d), 2 + i, term(4, first_q[d]), first_q[d], on_ring(2 * d))
            scatter(("a", d), i, term(3 * d), None, on_ring(d))
        def scatter_second():
            for i, d in ways:
                mid = (term(2 * d, 0), term(2 * d, 1))
                rs["a", d].wait_recv()
                near = [mid[q] + s["rs_recv"][i, :, cols(q)].astype(f32) for q in (0, 1)]
                near[first_q[d]] = near[first_q[d]] + landed(("b", d), 2 + i, first_q[d])
                scatter(("c", d), 4 + i, jnp.concatenate(near, axis=1), None, on_ring(2 * d))

        lo2()
        gather_near()

        @pl.when(sec < secs - 2)
        def _():
            sw_car.start()

        ld_mag.wait()
        norms = jnp.sqrt(sq3() + epsilon)
        s["norms"][...] = norms
        s["scale"][...] = mag[...] / norms

        sw_hb.wait_recv()
        rcols = min(512, width)
        n_rec = width // rcols

        def recompute(i, carry):
            cc = pl.ds(pl.multiple_of(i * rcols, rcols), rcols)
            s["rec"][:, cc] = dot(xb[...].reshape(2 * half_rows, depth), w[:, cc], 1, 0)
            return carry

        lax.fori_loop(0, n_rec, recompute, 0)
        s["low_own"][...] = lo3().astype(bf16)
        sw_low = remote(s["low_own"], s["low_oth"], partner)
        start(sw_low)
        gather_last()
        for i, d in ways:
            scatter(("d", d), 6 + i, term(d), None, on_ring(d))

        def rescale(i, carry):
            scot[i] = (cot[i].astype(f32) * s["scale"][...]).astype(bf16)
            return carry

        lax.fori_loop(0, tens, rescale, 0)

        def magnitudes(i, carry):
            cc = pl.ds(pl.multiple_of(i * step_cols, step_cols), step_cols)
            got = cot[:, :, cc].reshape(2 * half_rows, step_cols).astype(f32)
            part = jnp.sum((s["rec"][:, cc] * got).reshape(half_rows // 4, 8, step_cols), axis=0)
            s["gmp"][:, cc] = jnp.sum(part, axis=0, keepdims=True)
            return carry

        hsplit = [(0, 512), (512, depth - 512)]

        def hidden(which, lo, size):
            rows = scot[pl.ds(which * blocks, blocks)].reshape(half_rows, width)
            return dot(rows, w[pl.ds(lo, size), :], 1, 1)

        sw_hg = []
        for lo, size in hsplit:
            s["hg_send"][:, pl.ds(lo, size)] = hidden(1 - half, lo, size).astype(bf16)
            copy = remote(s["hg_send"].at[:, pl.ds(lo, size)], s["hg_recv"].at[:, pl.ds(lo, size)], partner)
            start(copy)
            sw_hg.append(copy)
            if lo == 0:
                lax.fori_loop(0, n_merge, magnitudes, 0)
                gm1()

        adapt = dot(b[...], scot[...].reshape(2 * half_rows, width), 1, 1)
        s["ad"][...] = adapt.reshape(2, 8, 2 * half_rows)
        sw_ad = remote(s["ad"].at[1 - half], s["ad_recv"], partner)
        start(sw_ad)

        scatter_second()
        gm2()

        for lo_, size_ in hsplit:
            s["hg_own"][:, pl.ds(lo_, size_)] = hidden(half, lo_, size_)

        sw_ad.wait_recv()
        own_ad = (s["ad"][half] + s["ad_recv"][...]).astype(bf16)
        s["ga"][...] = dot(own_ad, xb[...].reshape(2 * half_rows, depth), 1, 0)
        out_ga = local(s["ga"], ga_out.at[0])
        out_ga.start()
        sw_low.wait_recv()
        s["gb"][...] = dot(
            s["low_own"][...], scot[pl.ds(half * blocks, blocks)].reshape(half_rows, width), 1, 0
        ) + dot(
            s["low_oth"][...], scot[pl.ds((1 - half) * blocks, blocks)].reshape(half_rows, width), 1, 0
        )
        out_gb = local(s["gb"], gb_out.at[0])
        out_gb.start()

        s["gm"][...] = gm3() / s["norms"][...]
        out_gm = local(s["gm"], gm_out)
        out_gm.start()

        @pl.when(sec < 2)
        def _():
            ld_infl.wait()

        @pl.when(sec >= 2)
        def _():
            sw_car.wait_recv()

        val = term(0)
        for i, d in ways:
            val = val + landed(("d", d), 6 + i) + landed(("c", d), 4 + i)
        val = infl[...].astype(f32) + val * s["scale"][...]
        s["so"][...] = val.astype(bf16)
        out_so = local(s["so"], so_out.at[0])
        out_so.start()

        for copy in sw_hg:
            copy.wait_recv()
        s["hg"][...] = (s["hg_own"][...] + s["hg_recv"][...].astype(f32)).astype(bf16)
        out_hg = local(s["hg"], hg_out.at[0])
        out_hg.start()

        for copy in sent:
            copy.wait_send()

        @pl.when(sec >= 2)
        def _():
            sw_ret.wait_send()

        @pl.when(sec < secs - 2)
        def _():
            sw_car.wait_send()

        for copy in (out_ga, out_gb, out_so, out_gm, out_hg):
            copy.wait()

    return kernel


def hand_over(*refs):
    given, results, held, sems = refs[:5], refs[5:10], refs[10:15], refs[15]
    into = [pltpu.make_async_copy(given[i], held[i], sems.at[i]) for i in range(5)]
    out = [pltpu.make_async_copy(held[i], results[i], sems.at[5 + i]) for i in range(5)]
    for copy in into:
        copy.start()
    for i in range(5):
        into[i].wait()
        out[i].start()
    for copy in out:
        copy.wait()


def local(secs, tens, *args):
    (frozen, adapter_a, adapter_b, magnitude, hidden_fwd, carried, embedded, hidden_bwd, returned, head) = args
    depth, width = frozen.shape[1:]
    half_rows = hidden_fwd.shape[1]
    rings = tens // 2
    n_sems = 320
    shapes = {
        "w": pltpu.VMEM((depth, width), bf16),
        "a_own": pltpu.VMEM((8, depth), bf16),
        "a_oth": pltpu.VMEM((8, depth), bf16),
        "at": pltpu.VMEM((depth, 16), bf16),
        "b": pltpu.VMEM((16, width), bf16),
        "mag": pltpu.VMEM((1, width), f32),
        "norms": pltpu.VMEM((1, width), f32),
        "scale": pltpu.VMEM((1, width), f32),
        "xf": pltpu.VMEM((2, rings, 16, depth), bf16),
        "xb": pltpu.VMEM((2, half_rows, depth), bf16),
        "infl": pltpu.VMEM((16, width), bf16),
        "cot": pltpu.VMEM((tens, 16, width), bf16),
        "scot": pltpu.VMEM((tens, 16, width), bf16),
        "sq": pltpu.VMEM((1, width), f32),
        "sq_sib": pltpu.VMEM((1, width), f32),
        "sq_slots": pltpu.VMEM((rings, 1, width), f32),
        "gmp": pltpu.VMEM((1, width), f32),
        "gm_sib": pltpu.VMEM((1, width), f32),
        "gm_slots": pltpu.VMEM((rings, 1, width), f32),
        "lo": pltpu.VMEM((16, half_rows), f32),
        "lo_sib": pltpu.VMEM((16, half_rows), f32),
        "lo_slots": pltpu.VMEM((rings, 16, half_rows), f32),
        "low_own": pltpu.VMEM((16, half_rows), bf16),
        "low_oth": pltpu.VMEM((16, half_rows), bf16),
        "p_send": pltpu.VMEM((rings, 16, width), bf16),
        "p_recv": pltpu.VMEM((rings, 16, width), bf16),
        "pm": pltpu.VMEM((rings, 16, width), f32),
        "rs_send": pltpu.VMEM((8, 16, width), bf16),
        "rs_recv": pltpu.VMEM((8, 16, width), bf16),
        "rec": pltpu.VMEM((2 * half_rows, width), f32),
        "hg_send": pltpu.VMEM((half_rows, depth), bf16),
        "hg_recv": pltpu.VMEM((half_rows, depth), bf16),
        "hg_own": pltpu.VMEM((half_rows, depth), f32),
        "ad": pltpu.VMEM((2, 8, 2 * half_rows), f32),
        "ad_recv": pltpu.VMEM((8, 2 * half_rows), f32),
        "so": pltpu.VMEM((16, width), bf16),
        "gm": pltpu.VMEM((1, width), f32),
        "ga": pltpu.VMEM((8, depth), f32),
        "gb": pltpu.VMEM((16, width), f32),
        "hg": pltpu.VMEM((half_rows, depth), bf16),
        "sems": pltpu.SemaphoreType.DMA((n_sems,)),
    }
    anywhere = pl.BlockSpec(memory_space=pl.ANY)
    results = pl.pallas_call(
        make_kernel(secs, tens, list(shapes), n_sems),
        out_shape=(
            jax.ShapeDtypeStruct((1, 16, width), bf16),
            jax.ShapeDtypeStruct((1, width), f32),
            jax.ShapeDtypeStruct((1, 8, depth), f32),
            jax.ShapeDtypeStruct((1, 16, width), f32),
            jax.ShapeDtypeStruct((1, half_rows, depth), bf16),
        ),
        in_specs=[anywhere] * 10,
        out_specs=(anywhere,) * 5,
        scratch_shapes=list(shapes.values()),
        compiler_params=pltpu.CompilerParams(
            collective_id=0, has_side_effects=True, vmem_limit_bytes=63 * 1024 * 1024
        ),
    )(
        frozen,
        adapter_a,
        adapter_b,
        magnitude,
        hidden_fwd.reshape(half_rows // 32, 2, 16, depth),
        carried,
        embedded,
        hidden_bwd,
        returned,
        head,
    )
    return pl.pallas_call(
        hand_over,
        out_shape=[jax.ShapeDtypeStruct(r.shape, r.dtype) for r in results],
        in_specs=[anywhere] * 5,
        out_specs=[anywhere] * 5,
        scratch_shapes=[pltpu.VMEM(r.shape, r.dtype) for r in results] + [pltpu.SemaphoreType.DMA((10,))],
        compiler_params=pltpu.CompilerParams(vmem_limit_bytes=63 * 1024 * 1024),
    )(*results)


def solution(mesh):
    secs, tens = mesh.shape["section"], mesh.shape["tensor"]
    placed = (
        P("section", "tensor", None),
        P("section", None, "tensor"),
        P("section", None, None),
        P("section", None),
        P("section", None, "tensor"),
        P("section", "tensor", None),
        P("tensor", None),
        P("section", None, "tensor"),
        P("section", "tensor", None),
        P("tensor", None),
    )

    def run(*args):
        return local(secs, tens, *args)

    return jax.shard_map(
        run,
        mesh=mesh,
        in_specs=placed,
        out_specs=(
            P("section", "tensor", None),
            P("section", None),
            P("section", None, "tensor"),
            P("section", None, None),
            P("section", None, "tensor"),
        ),
        check_vma=False,
    )
```

```python
import jax
import jax.numpy as jnp
from jax import lax
from jax.experimental import pallas as pl
from jax.experimental.pallas import tpu as pltpu
from jax.sharding import PartitionSpec as P

epsilon = 1e-06
bf16 = jnp.bfloat16
f32 = jnp.float32


def dot(left, right, left_dim, right_dim):
    return lax.dot_general(
        left, right, (((left_dim,), (right_dim,)), ((), ())), preferred_element_type=f32
    )


def make_kernel(secs, tens, names, n_sems):
    rings = tens // 2
    assert rings == 8

    def kernel(*refs):
        (w_in, a_in, b_in, mag_in, hf_in, car_in, emb_in, hb_in, ret_in, head_in) = refs[:10]
        (so_out, gm_out, ga_out, gb_out, hg_out) = refs[10:15]
        s = dict(zip(names, refs[15:]))
        w, a_own, a_oth, b, mag = s["w"], s["a_own"], s["a_oth"], s["b"], s["mag"]
        xf, xb, infl, cot, scot = s["xf"], s["xb"], s["infl"], s["cot"], s["scot"]
        sems = s["sems"]
        used = [0]

        def sem():
            used[0] += 1
            assert used[0] <= n_sems
            return sems.at[used[0] - 1]

        depth, width = w.shape
        wide = width // 2
        half_rows = xb.shape[1]
        blocks = half_rows // 16

        sec = lax.axis_index("section")
        ten = lax.axis_index("tensor")
        half = lax.rem(sec, 2)
        core = lax.rem(ten, 2)
        z = ten // 2
        partner = {"section": sec + 1 - 2 * half}
        sibling = {"tensor": ten + 1 - 2 * core}
        next_sec = {"section": lax.rem(sec + 2, secs)}
        prev_sec = {"section": lax.rem(sec + secs - 2, secs)}

        def remote(src, dst, where):
            return pltpu.make_async_remote_copy(
                src_ref=src,
                dst_ref=dst,
                send_sem=sem(),
                recv_sem=sem(),
                device_id=where,
                device_id_type=pl.DeviceIdType.MESH,
            )

        def local(src, dst):
            return pltpu.make_async_copy(src, dst, sem())

        def cols(q):
            return pl.ds(q * wide, wide)

        sent = []

        def start(*copies):
            for copy in copies:
                copy.start()
                sent.append(copy)

        ld_a = local(a_in.at[0], a_own)
        ld_b = local(b_in.at[0], b)
        ld_w = local(w_in.at[0], w)
        ld_mag = local(mag_in, mag)
        ld_hb = local(hb_in.at[0], xb.at[half])
        ld_hf = [local(hf_in.at[:, p], xf.at[p, pl.ds(half * (blocks // 2), blocks // 2)]) for p in (0, 1)]
        own_cols = pl.ds(pl.multiple_of(half * width, 128), width)
        ld_infl = local(emb_in.at[:, own_cols], infl)
        ld_cot = local(head_in.at[:, own_cols], cot.at[ten])
        for copy in (ld_a, ld_b, ld_w, ld_hb, ld_mag, *ld_hf):
            copy.start()

        @pl.when(sec < 2)
        def _():
            ld_infl.start()

        @pl.when(sec >= secs - 2)
        def _():
            ld_cot.start()

        barrier = pltpu.get_barrier_semaphore()
        peers = [{"tensor": lax.rem(ten + k, tens)} for k in range(1, tens)]
        everyone = [partner, next_sec, prev_sec] + peers
        for where in everyone:
            pl.semaphore_signal(barrier, inc=1, device_id=where, device_id_type=pl.DeviceIdType.MESH)
        pl.semaphore_wait(barrier, len(everyone))

        sw_a = remote(a_in.at[0], a_oth, partner)
        sw_ret = remote(ret_in.at[0], cot.at[ten], prev_sec)
        sw_hf = [
            remote(hf_in.at[:, p], xf.at[p, pl.ds(half * (blocks // 2), blocks // 2)], partner)
            for p in (0, 1)
        ]
        sw_hb = remote(hb_in.at[0], xb.at[half], partner)
        sw_car = remote(car_in.at[0], infl, next_sec)
        start(sw_a)

        @pl.when(sec >= 2)
        def _():
            sw_ret.start()

        def at_ring(k):
            return lax.rem(z + k + rings, rings)

        def on_ring(k):
            return {"tensor": at_ring(k) * 2 + core}

        def cot_copy(k, q, where):
            ref = cot.at[at_ring(k) * 2 + core]
            if q is not None:
                ref = cot.at[at_ring(k) * 2 + core, :, cols(q)]
            return remote(ref, ref, where)

        first_q = {1: 0, -1: 1}
        ag_own = {k: cot_copy(0, None, on_ring(k)) for k in (2, -2, 1, -1)}
        ag_far = {}
        ag_x = []

        def cross(k):
            ag_x.append(cot_copy(k, None, sibling))
            start(ag_x[-1])

        def gather_first():
            @pl.when(sec < secs - 2)
            def _():
                sw_ret.wait_recv()

            @pl.when(sec >= secs - 2)
            def _():
                ld_cot.wait()

            start(*ag_own.values())
            cross(0)

        def gather_second():
            for d in (1, -1):
                ag_own[2 * d].wait_recv()
                ag_far[3 * d] = cot_copy(-2 * d, None, on_ring(d))
                ag_far[4 * d] = cot_copy(-2 * d, first_q[d], on_ring(2 * d))
                start(ag_far[3 * d], ag_far[4 * d])
                cross(-2 * d)

        def gather_near():
            for d in (1, -1):
                ag_own[d].wait_recv()
                cross(-d)

        def gather_last():
            for d in (1, -1):
                ag_far[3 * d].wait_recv()
                cross(-3 * d)
            for d in (1, -1):
                ag_far[4 * d].wait_recv()
            cross(4)
            for copy in ag_x:
                copy.wait_recv()

        def total_of(part, sib, slots, own_half):
            first = remote(part, sib, sibling)

            def stage1():
                start(first)

            copies = []

            def stage2():
                first.wait_recv()
                slots[z] = part[...] + sib[...]
                ref = slots.at[(z, *own_half)]
                for k in range(1, rings):
                    for other in (0, 1):
                        there = lax.rem(z + k, rings) * 2 + (core if other == 0 else 1 - core)
                        copies.append(remote(ref, ref, {"tensor": there}))
                start(*copies)

            def stage3():
                for copy in copies:
                    copy.wait_recv()
                total = slots[0]
                for k in range(1, rings):
                    total = total + slots[k]
                return total

            return stage1, stage2, stage3

        lane_half = (slice(None), pl.ds(pl.multiple_of(core * wide, 128), wide))
        row_half = (pl.ds(pl.multiple_of(core * 8, 8), 8), slice(None))
        sq1, sq2, sq3 = total_of(s["sq"], s["sq_sib"], s["sq_slots"], lane_half)
        gm1, gm2, gm3 = total_of(s["gmp"], s["gm_sib"], s["gm_slots"], lane_half)
        lo1, lo2, lo3 = total_of(s["lo"], s["lo_sib"], s["lo_slots"], row_half)

        ld_a.wait()
        ld_b.wait()
        sw_a.wait_recv()
        start(*sw_hf)
        mine, theirs = a_own[...].astype(f32), a_oth[...].astype(f32)
        first = half == 0
        a_all = jnp.concatenate(
            [jnp.where(first, mine, theirs), jnp.where(first, theirs, mine)], axis=0
        )
        s["at"][...] = a_all.T.astype(bf16)

        step_cols = min(256, width)
        step_rows = min(128, depth)

        def merge(i, carry):
            cc = pl.ds(pl.multiple_of(i * step_cols, step_cols), step_cols)
            b_c = b[:, cc]
            total = jnp.zeros((8, step_cols), f32)
            for r in range(0, depth, step_rows):
                rr = pl.ds(r, step_rows)
                m = (w[rr, cc].astype(f32) + dot(s["at"][rr, :], b_c, 1, 0)).astype(bf16)
                w[rr, cc] = m
                m = m.astype(f32)
                total = total + jnp.sum((m * m).reshape(step_rows // 8, 8, step_cols), axis=0)
            s["sq"][:, cc] = jnp.sum(total, axis=0, keepdims=True)
            return carry

        ld_w.wait()
        n_merge = width // step_cols
        lax.fori_loop(0, n_merge * 5 // 8, merge, 0)
        gather_first()
        lax.fori_loop(n_merge * 5 // 8, n_merge, merge, 0)
        sq1()

        ld_hb.wait()
        s["lo"][...] = dot(a_all.astype(bf16), xb[half], 1, 1)
        lo1()
        sq2()

        for copy in ld_hf:
            copy.wait()
        for copy in sw_hf:
            copy.wait_recv()
        start(sw_hb)

        pcols = min(512, width)

        def project(parity, keep, lo, hi):
            def body(i, carry):
                cc = pl.ds(pl.multiple_of(i * pcols, pcols), pcols)
                x = xf[parity].reshape(half_rows, depth)
                res = dot(x, w[:, cc], 1, 0)
                keep[:, :, cc] = res.reshape(rings, 16, pcols).astype(keep.dtype)
                return carry

            lax.fori_loop(lo // pcols, hi // pcols, body, 0)

        sw_p = []
        for q in (0, 1):
            project(1 - core, s["p_send"], q * wide, (q + 1) * wide)
            sw_p.append(remote(s["p_send"].at[:, :, cols(q)], s["p_recv"].at[:, :, cols(q)], sibling))
            start(sw_p[q])
        gather_second()
        project(core, s["pm"], 0, width)
        for copy in sw_p:
            copy.wait_recv()

        pm = s["pm"]

        def term(k, q=None):
            cc = slice(None) if q is None else cols(q)
            return pm[at_ring(k), :, cc] + s["p_recv"][at_ring(k), :, cc].astype(f32)

        rs = {}

        def scatter(name, slot, val, q, where):
            cc = slice(None) if q is None else cols(q)
            s["rs_send"][slot, :, cc] = val.astype(bf16)
            copy = remote(s["rs_send"].at[slot, :, cc], s["rs_recv"].at[slot, :, cc], where)
            start(copy)
            rs[name] = copy

        def landed(name, slot, q=None):
            cc = slice(None) if q is None else cols(q)
            rs[name].wait_recv()
            return s["rs_recv"][slot, :, cc].astype(f32)

        ways = ((0, 1), (1, -1))
        for i, d in ways:
            scatter(("b", d), 2 + i, term(4, first_q[d]), first_q[d], on_ring(2 * d))
            scatter(("a", d), i, term(3 * d), None, on_ring(d))
        def scatter_second():
            for i, d in ways:
                mid = (term(2 * d, 0), term(2 * d, 1))
                rs["a", d].wait_recv()
                near = [mid[q] + s["rs_recv"][i, :, cols(q)].astype(f32) for q in (0, 1)]
                near[first_q[d]] = near[first_q[d]] + landed(("b", d), 2 + i, first_q[d])
                scatter(("c", d), 4 + i, jnp.concatenate(near, axis=1), None, on_ring(2 * d))

        gather_near()

        ld_mag.wait()
        norms = jnp.sqrt(sq3() + epsilon)
        s["norms"][...] = norms
        s["scale"][...] = mag[...] / norms

        sw_hb.wait_recv()
        rcols = min(512, width)
        n_rec = width // rcols

        def recompute(i, carry):
            cc = pl.ds(pl.multiple_of(i * rcols, rcols), rcols)
            s["rec"][:, cc] = dot(xb[...].reshape(2 * half_rows, depth), w[:, cc], 1, 0)
            return carry

        lax.fori_loop(0, n_rec, recompute, 0)
        gather_last()
        lo2()
        for i, d in ways:
            scatter(("d", d), 6 + i, term(d), None, on_ring(d))

        def rescale(i, carry):
            scot[i] = (cot[i].astype(f32) * s["scale"][...]).astype(bf16)
            return carry

        lax.fori_loop(0, tens, rescale, 0)

        def magnitudes(i, carry):
            cc = pl.ds(pl.multiple_of(i * step_cols, step_cols), step_cols)
            got = cot[:, :, cc].reshape(2 * half_rows, step_cols).astype(f32)
            part = jnp.sum((s["rec"][:, cc] * got).reshape(half_rows // 4, 8, step_cols), axis=0)
            s["gmp"][:, cc] = jnp.sum(part, axis=0, keepdims=True)
            return carry

        lax.fori_loop(0, n_merge, magnitudes, 0)
        gm1()

        hsplit = [(0, 512), (512, depth - 512)]

        def hidden(which, lo, size):
            rows = scot[pl.ds(which * blocks, blocks)].reshape(half_rows, width)
            return dot(rows, w[pl.ds(lo, size), :], 1, 1)

        sw_hg = []
        for lo, size in hsplit:
            s["hg_send"][:, pl.ds(lo, size)] = hidden(1 - half, lo, size).astype(bf16)
            copy = remote(s["hg_send"].at[:, pl.ds(lo, size)], s["hg_recv"].at[:, pl.ds(lo, size)], partner)
            start(copy)
            sw_hg.append(copy)
            if lo == 0:
                gm2()

        @pl.when(sec < secs - 2)
        def _():
            sw_car.start()

        adapt = dot(b[...], scot[...].reshape(2 * half_rows, width), 1, 1)
        s["ad"][...] = adapt.reshape(2, 8, 2 * half_rows)
        sw_ad = remote(s["ad"].at[1 - half], s["ad_recv"], partner)
        start(sw_ad)

        scatter_second()

        for lo_, size_ in hsplit:
            s["hg_own"][:, pl.ds(lo_, size_)] = hidden(half, lo_, size_)

        s["low_own"][...] = lo3().astype(bf16)
        sw_low = remote(s["low_own"], s["low_oth"], partner)
        start(sw_low)
        sw_ad.wait_recv()
        own_ad = (s["ad"][half] + s["ad_recv"][...]).astype(bf16)
        s["ga"][...] = dot(own_ad, xb[...].reshape(2 * half_rows, depth), 1, 0)
        out_ga = local(s["ga"], ga_out.at[0])
        out_ga.start()
        sw_low.wait_recv()
        s["gb"][...] = dot(
            s["low_own"][...], scot[pl.ds(half * blocks, blocks)].reshape(half_rows, width), 1, 0
        ) + dot(
            s["low_oth"][...], scot[pl.ds((1 - half) * blocks, blocks)].reshape(half_rows, width), 1, 0
        )
        out_gb = local(s["gb"], gb_out.at[0])
        out_gb.start()

        s["gm"][...] = gm3() / s["norms"][...]
        out_gm = local(s["gm"], gm_out)
        out_gm.start()

        @pl.when(sec < 2)
        def _():
            ld_infl.wait()

        @pl.when(sec >= 2)
        def _():
            sw_car.wait_recv()

        val = term(0)
        for i, d in ways:
            val = val + landed(("d", d), 6 + i) + landed(("c", d), 4 + i)
        val = infl[...].astype(f32) + val * s["scale"][...]
        s["so"][...] = val.astype(bf16)
        out_so = local(s["so"], so_out.at[0])
        out_so.start()

        for copy in sw_hg:
            copy.wait_recv()
        s["hg"][...] = (s["hg_own"][...] + s["hg_recv"][...].astype(f32)).astype(bf16)
        out_hg = local(s["hg"], hg_out.at[0])
        out_hg.start()

        for copy in sent:
            copy.wait_send()

        @pl.when(sec >= 2)
        def _():
            sw_ret.wait_send()

        @pl.when(sec < secs - 2)
        def _():
            sw_car.wait_send()

        for copy in (out_ga, out_gb, out_so, out_gm, out_hg):
            copy.wait()

    return kernel


def hand_over(*refs):
    given, results, held, sems = refs[:5], refs[5:10], refs[10:15], refs[15]
    into = [pltpu.make_async_copy(given[i], held[i], sems.at[i]) for i in range(5)]
    out = [pltpu.make_async_copy(held[i], results[i], sems.at[5 + i]) for i in range(5)]
    for copy in into:
        copy.start()
    for i in range(5):
        into[i].wait()
        out[i].start()
    for copy in out:
        copy.wait()


def local(secs, tens, *args):
    (frozen, adapter_a, adapter_b, magnitude, hidden_fwd, carried, embedded, hidden_bwd, returned, head) = args
    depth, width = frozen.shape[1:]
    half_rows = hidden_fwd.shape[1]
    rings = tens // 2
    n_sems = 320
    shapes = {
        "w": pltpu.VMEM((depth, width), bf16),
        "a_own": pltpu.VMEM((8, depth), bf16),
        "a_oth": pltpu.VMEM((8, depth), bf16),
        "at": pltpu.VMEM((depth, 16), bf16),
        "b": pltpu.VMEM((16, width), bf16),
        "mag": pltpu.VMEM((1, width), f32),
        "norms": pltpu.VMEM((1, width), f32),
        "scale": pltpu.VMEM((1, width), f32),
        "xf": pltpu.VMEM((2, rings, 16, depth), bf16),
        "xb": pltpu.VMEM((2, half_rows, depth), bf16),
        "infl": pltpu.VMEM((16, width), bf16),
        "cot": pltpu.VMEM((tens, 16, width), bf16),
        "scot": pltpu.VMEM((tens, 16, width), bf16),
        "sq": pltpu.VMEM((1, width), f32),
        "sq_sib": pltpu.VMEM((1, width), f32),
        "sq_slots": pltpu.VMEM((rings, 1, width), f32),
        "gmp": pltpu.VMEM((1, width), f32),
        "gm_sib": pltpu.VMEM((1, width), f32),
        "gm_slots": pltpu.VMEM((rings, 1, width), f32),
        "lo": pltpu.VMEM((16, half_rows), f32),
        "lo_sib": pltpu.VMEM((16, half_rows), f32),
        "lo_slots": pltpu.VMEM((rings, 16, half_rows), f32),
        "low_own": pltpu.VMEM((16, half_rows), bf16),
        "low_oth": pltpu.VMEM((16, half_rows), bf16),
        "p_send": pltpu.VMEM((rings, 16, width), bf16),
        "p_recv": pltpu.VMEM((rings, 16, width), bf16),
        "pm": pltpu.VMEM((rings, 16, width), f32),
        "rs_send": pltpu.VMEM((8, 16, width), bf16),
        "rs_recv": pltpu.VMEM((8, 16, width), bf16),
        "rec": pltpu.VMEM((2 * half_rows, width), f32),
        "hg_send": pltpu.VMEM((half_rows, depth), bf16),
        "hg_recv": pltpu.VMEM((half_rows, depth), bf16),
        "hg_own": pltpu.VMEM((half_rows, depth), f32),
        "ad": pltpu.VMEM((2, 8, 2 * half_rows), f32),
        "ad_recv": pltpu.VMEM((8, 2 * half_rows), f32),
        "so": pltpu.VMEM((16, width), bf16),
        "gm": pltpu.VMEM((1, width), f32),
        "ga": pltpu.VMEM((8, depth), f32),
        "gb": pltpu.VMEM((16, width), f32),
        "hg": pltpu.VMEM((half_rows, depth), bf16),
        "sems": pltpu.SemaphoreType.DMA((n_sems,)),
    }
    anywhere = pl.BlockSpec(memory_space=pl.ANY)
    results = pl.pallas_call(
        make_kernel(secs, tens, list(shapes), n_sems),
        out_shape=(
            jax.ShapeDtypeStruct((1, 16, width), bf16),
            jax.ShapeDtypeStruct((1, width), f32),
            jax.ShapeDtypeStruct((1, 8, depth), f32),
            jax.ShapeDtypeStruct((1, 16, width), f32),
            jax.ShapeDtypeStruct((1, half_rows, depth), bf16),
        ),
        in_specs=[anywhere] * 10,
        out_specs=(anywhere,) * 5,
        scratch_shapes=list(shapes.values()),
        compiler_params=pltpu.CompilerParams(
            collective_id=0, has_side_effects=True, vmem_limit_bytes=63 * 1024 * 1024
        ),
    )(
        frozen,
        adapter_a,
        adapter_b,
        magnitude,
        hidden_fwd.reshape(half_rows // 32, 2, 16, depth),
        carried,
        embedded,
        hidden_bwd,
        returned,
        head,
    )
    return pl.pallas_call(
        hand_over,
        out_shape=[jax.ShapeDtypeStruct(r.shape, r.dtype) for r in results],
        in_specs=[anywhere] * 5,
        out_specs=[anywhere] * 5,
        scratch_shapes=[pltpu.VMEM(r.shape, r.dtype) for r in results] + [pltpu.SemaphoreType.DMA((10,))],
        compiler_params=pltpu.CompilerParams(vmem_limit_bytes=63 * 1024 * 1024),
    )(*results)


def solution(mesh):
    secs, tens = mesh.shape["section"], mesh.shape["tensor"]
    placed = (
        P("section", "tensor", None),
        P("section", None, "tensor"),
        P("section", None, None),
        P("section", None),
        P("section", None, "tensor"),
        P("section", "tensor", None),
        P("tensor", None),
        P("section", None, "tensor"),
        P("section", "tensor", None),
        P("tensor", None),
    )

    def run(*args):
        return local(secs, tens, *args)

    return jax.shard_map(
        run,
        mesh=mesh,
        in_specs=placed,
        out_specs=(
            P("section", "tensor", None),
            P("section", None),
            P("section", None, "tensor"),
            P("section", None, None),
            P("section", None, "tensor"),
        ),
        check_vma=False,
    )
```

```python
import jax
import jax.numpy as jnp
from jax import lax
from jax.experimental import pallas as pl
from jax.experimental.pallas import tpu as pltpu
from jax.sharding import PartitionSpec as P

epsilon = 1e-06
bf16 = jnp.bfloat16
f32 = jnp.float32


def dot(left, right, left_dim, right_dim):
    return lax.dot_general(
        left, right, (((left_dim,), (right_dim,)), ((), ())), preferred_element_type=f32
    )


def make_kernel(secs, tens, names, n_sems):
    rings = tens // 2
    assert rings == 8

    def kernel(*refs):
        (w_in, a_in, b_in, mag_in, hf_in, car_in, emb_in, hb_in, ret_in, head_in) = refs[:10]
        (so_out, gm_out, ga_out, gb_out, hg_out) = refs[10:15]
        s = dict(zip(names, refs[15:]))
        w, a_own, a_oth, b, mag = s["w"], s["a_own"], s["a_oth"], s["b"], s["mag"]
        xf, xb, infl, cot, scot = s["xf"], s["xb"], s["infl"], s["cot"], s["scot"]
        sems = s["sems"]
        used = [0]

        def sem():
            used[0] += 1
            assert used[0] <= n_sems
            return sems.at[used[0] - 1]

        depth, width = w.shape
        wide = width // 2
        half_rows = xb.shape[1]
        blocks = half_rows // 16

        sec = lax.axis_index("section")
        ten = lax.axis_index("tensor")
        half = lax.rem(sec, 2)
        core = lax.rem(ten, 2)
        z = ten // 2
        partner = {"section": sec + 1 - 2 * half}
        sibling = {"tensor": ten + 1 - 2 * core}
        next_sec = {"section": lax.rem(sec + 2, secs)}
        prev_sec = {"section": lax.rem(sec + secs - 2, secs)}

        def remote(src, dst, where):
            return pltpu.make_async_remote_copy(
                src_ref=src,
                dst_ref=dst,
                send_sem=sem(),
                recv_sem=sem(),
                device_id=where,
                device_id_type=pl.DeviceIdType.MESH,
            )

        def local(src, dst):
            return pltpu.make_async_copy(src, dst, sem())

        def cols(q):
            return pl.ds(q * wide, wide)

        sent = []

        def start(*copies):
            for copy in copies:
                copy.start()
                sent.append(copy)

        ld_a = local(a_in.at[0], a_own)
        ld_b = local(b_in.at[0], b)
        ld_w = local(w_in.at[0], w)
        ld_mag = local(mag_in, mag)
        ld_hb = local(hb_in.at[0], xb.at[half])
        ld_hf = [local(hf_in.at[:, p], xf.at[p, pl.ds(half * (blocks // 2), blocks // 2)]) for p in (0, 1)]
        own_cols = pl.ds(pl.multiple_of(half * width, 128), width)
        ld_infl = local(emb_in.at[:, own_cols], infl)
        ld_cot = local(head_in.at[:, own_cols], cot.at[ten])
        for copy in (ld_a, ld_b, ld_w, ld_hb, ld_mag, *ld_hf):
            copy.start()

        @pl.when(sec < 2)
        def _():
            ld_infl.start()

        @pl.when(sec >= secs - 2)
        def _():
            ld_cot.start()

        barrier = pltpu.get_barrier_semaphore()
        peers = [{"tensor": lax.rem(ten + k, tens)} for k in range(1, tens)]
        everyone = [partner, next_sec, prev_sec] + peers
        for where in everyone:
            pl.semaphore_signal(barrier, inc=1, device_id=where, device_id_type=pl.DeviceIdType.MESH)
        pl.semaphore_wait(barrier, len(everyone))

        sw_a = remote(a_in.at[0], a_oth, partner)
        sw_ret = [remote(ret_in.at[0, :, cols(q)], cot.at[ten, :, cols(q)], prev_sec) for q in (0, 1)]
        sw_hf = [
            remote(hf_in.at[:, p], xf.at[p, pl.ds(half * (blocks // 2), blocks // 2)], partner)
            for p in (0, 1)
        ]
        sw_hb = remote(hb_in.at[0], xb.at[half], partner)
        sw_car = remote(car_in.at[0], infl, next_sec)
        start(sw_a)

        @pl.when(sec >= 2)
        def _():
            for copy in sw_ret:
                copy.start()

        def at_ring(k):
            return lax.rem(z + k + rings, rings)

        def on_ring(k):
            return {"tensor": at_ring(k) * 2 + core}

        def cot_copy(k, q, where):
            ref = cot.at[at_ring(k) * 2 + core]
            if q is not None:
                ref = cot.at[at_ring(k) * 2 + core, :, cols(q)]
            return remote(ref, ref, where)

        first_q = {1: 0, -1: 1}
        ag_own = {(k, q): cot_copy(0, q, on_ring(k)) for q in (0, 1) for k in (2, -2, 1, -1)}
        ag_far = {}
        ag_x = []

        def cross(k):
            ag_x.append(cot_copy(k, None, sibling))
            start(ag_x[-1])

        def gather_first():
            @pl.when(sec >= secs - 2)
            def _():
                ld_cot.wait()

            for q in (0, 1):

                @pl.when(sec < secs - 2)
                def _():
                    sw_ret[q].wait_recv()

                start(*[ag_own[k, q] for k in (2, -2, 1, -1)])
            cross(0)

        def gather_second(q):
            for d in (1, -1):
                ag_own[2 * d, q].wait_recv()
                ag_far[3 * d, q] = cot_copy(-2 * d, q, on_ring(d))
                start(ag_far[3 * d, q])
                if q == first_q[d]:
                    ag_far[4 * d] = cot_copy(-2 * d, q, on_ring(2 * d))
                    start(ag_far[4 * d])
                if q == 1:
                    cross(-2 * d)

        def gather_near():
            for d in (1, -1):
                for q in (0, 1):
                    ag_own[d, q].wait_recv()
                cross(-d)

        def gather_last():
            for d in (1, -1):
                for q in (0, 1):
                    ag_far[3 * d, q].wait_recv()
                cross(-3 * d)
            for d in (1, -1):
                ag_far[4 * d].wait_recv()
            cross(4)
            for copy in ag_x:
                copy.wait_recv()

        def total_of(part, sib, slots, own_half):
            first = remote(part, sib, sibling)

            def stage1():
                start(first)

            copies = []

            def stage2():
                first.wait_recv()
                slots[z] = part[...] + sib[...]
                ref = slots.at[(z, *own_half)]
                for k in range(1, rings):
                    for other in (0, 1):
                        there = lax.rem(z + k, rings) * 2 + (core if other == 0 else 1 - core)
                        copies.append(remote(ref, ref, {"tensor": there}))
                start(*copies)

            def stage3():
                for copy in copies:
                    copy.wait_recv()
                total = slots[0]
                for k in range(1, rings):
                    total = total + slots[k]
                return total

            return stage1, stage2, stage3

        lane_half = (slice(None), pl.ds(pl.multiple_of(core * wide, 128), wide))
        row_half = (pl.ds(pl.multiple_of(core * 8, 8), 8), slice(None))
        sq1, sq2, sq3 = total_of(s["sq"], s["sq_sib"], s["sq_slots"], lane_half)
        gm1, gm2, gm3 = total_of(s["gmp"], s["gm_sib"], s["gm_slots"], lane_half)
        lo1, lo2, lo3 = total_of(s["lo"], s["lo_sib"], s["lo_slots"], row_half)

        ld_a.wait()
        ld_b.wait()
        sw_a.wait_recv()
        start(*sw_hf)
        mine, theirs = a_own[...].astype(f32), a_oth[...].astype(f32)
        first = half == 0
        a_all = jnp.concatenate(
            [jnp.where(first, mine, theirs), jnp.where(first, theirs, mine)], axis=0
        )
        s["at"][...] = a_all.T.astype(bf16)

        step_cols = min(256, width)
        step_rows = min(128, depth)

        def merge(i, carry):
            cc = pl.ds(pl.multiple_of(i * step_cols, step_cols), step_cols)
            b_c = b[:, cc]
            total = jnp.zeros((8, step_cols), f32)
            for r in range(0, depth, step_rows):
                rr = pl.ds(r, step_rows)
                m = (w[rr, cc].astype(f32) + dot(s["at"][rr, :], b_c, 1, 0)).astype(bf16)
                w[rr, cc] = m
                m = m.astype(f32)
                total = total + jnp.sum((m * m).reshape(step_rows // 8, 8, step_cols), axis=0)
            s["sq"][:, cc] = jnp.sum(total, axis=0, keepdims=True)
            return carry

        ld_w.wait()
        n_merge = width // step_cols
        lax.fori_loop(0, n_merge * 5 // 8, merge, 0)
        gather_first()
        lax.fori_loop(n_merge * 5 // 8, n_merge, merge, 0)
        sq1()

        ld_hb.wait()
        s["lo"][...] = dot(a_all.astype(bf16), xb[half], 1, 1)
        lo1()
        sq2()

        for copy in ld_hf:
            copy.wait()
        for copy in sw_hf:
            copy.wait_recv()
        start(sw_hb)

        pcols = min(512, width)

        def project(parity, keep, lo, hi):
            def body(i, carry):
                cc = pl.ds(pl.multiple_of(i * pcols, pcols), pcols)
                x = xf[parity].reshape(half_rows, depth)
                res = dot(x, w[:, cc], 1, 0)
                keep[:, :, cc] = res.reshape(rings, 16, pcols).astype(keep.dtype)
                return carry

            lax.fori_loop(lo // pcols, hi // pcols, body, 0)

        gather_second(0)
        sw_p = []
        for q in (0, 1):
            project(1 - core, s["p_send"], q * wide, (q + 1) * wide)
            sw_p.append(remote(s["p_send"].at[:, :, cols(q)], s["p_recv"].at[:, :, cols(q)], sibling))
            start(sw_p[q])
        gather_second(1)
        project(core, s["pm"], 0, width)
        for copy in sw_p:
            copy.wait_recv()

        pm = s["pm"]

        def term(k, q=None):
            cc = slice(None) if q is None else cols(q)
            return pm[at_ring(k), :, cc] + s["p_recv"][at_ring(k), :, cc].astype(f32)

        rs = {}

        def scatter(name, slot, val, q, where):
            cc = slice(None) if q is None else cols(q)
            s["rs_send"][slot, :, cc] = val.astype(bf16)
            copy = remote(s["rs_send"].at[slot, :, cc], s["rs_recv"].at[slot, :, cc], where)
            start(copy)
            rs[name] = copy

        def landed(name, slot, q=None):
            cc = slice(None) if q is None else cols(q)
            rs[name].wait_recv()
            return s["rs_recv"][slot, :, cc].astype(f32)

        ways = ((0, 1), (1, -1))
        for i, d in ways:
            scatter(("b", d), 2 + i, term(4, first_q[d]), first_q[d], on_ring(2 * d))
            scatter(("a", d), i, term(3 * d), None, on_ring(d))
        def scatter_second():
            for i, d in ways:
                mid = (term(2 * d, 0), term(2 * d, 1))
                rs["a", d].wait_recv()
                near = [mid[q] + s["rs_recv"][i, :, cols(q)].astype(f32) for q in (0, 1)]
                near[first_q[d]] = near[first_q[d]] + landed(("b", d), 2 + i, first_q[d])
                scatter(("c", d), 4 + i, jnp.concatenate(near, axis=1), None, on_ring(2 * d))

        gather_near()

        ld_mag.wait()
        norms = jnp.sqrt(sq3() + epsilon)
        s["norms"][...] = norms
        s["scale"][...] = mag[...] / norms

        sw_hb.wait_recv()
        rcols = min(512, width)
        n_rec = width // rcols

        def recompute(i, carry):
            cc = pl.ds(pl.multiple_of(i * rcols, rcols), rcols)
            s["rec"][:, cc] = dot(xb[...].reshape(2 * half_rows, depth), w[:, cc], 1, 0)
            return carry

        lax.fori_loop(0, n_rec, recompute, 0)
        gather_last()
        lo2()
        for i, d in ways:
            scatter(("d", d), 6 + i, term(d), None, on_ring(d))

        def rescale(i, carry):
            scot[i] = (cot[i].astype(f32) * s["scale"][...]).astype(bf16)
            return carry

        lax.fori_loop(0, tens, rescale, 0)

        def magnitudes(i, carry):
            cc = pl.ds(pl.multiple_of(i * step_cols, step_cols), step_cols)
            got = cot[:, :, cc].reshape(2 * half_rows, step_cols).astype(f32)
            part = jnp.sum((s["rec"][:, cc] * got).reshape(half_rows // 4, 8, step_cols), axis=0)
            s["gmp"][:, cc] = jnp.sum(part, axis=0, keepdims=True)
            return carry

        lax.fori_loop(0, n_merge, magnitudes, 0)
        gm1()

        hsplit = [(0, 512), (512, depth - 512)]

        def hidden(which, lo, size):
            rows = scot[pl.ds(which * blocks, blocks)].reshape(half_rows, width)
            return dot(rows, w[pl.ds(lo, size), :], 1, 1)

        sw_hg = []
        for lo, size in hsplit:
            s["hg_send"][:, pl.ds(lo, size)] = hidden(1 - half, lo, size).astype(bf16)
            copy = remote(s["hg_send"].at[:, pl.ds(lo, size)], s["hg_recv"].at[:, pl.ds(lo, size)], partner)
            start(copy)
            sw_hg.append(copy)
            if lo == 0:
                gm2()
                scatter_second()

        @pl.when(sec < secs - 2)
        def _():
            sw_car.start()

        adapt = dot(b[...], scot[...].reshape(2 * half_rows, width), 1, 1)
        s["ad"][...] = adapt.reshape(2, 8, 2 * half_rows)
        sw_ad = remote(s["ad"].at[1 - half], s["ad_recv"], partner)
        start(sw_ad)


        for lo_, size_ in hsplit:
            s["hg_own"][:, pl.ds(lo_, size_)] = hidden(half, lo_, size_)

        s["low_own"][...] = lo3().astype(bf16)
        sw_low = remote(s["low_own"], s["low_oth"], partner)
        start(sw_low)
        sw_ad.wait_recv()
        own_ad = (s["ad"][half] + s["ad_recv"][...]).astype(bf16)
        ga_out[0] = dot(own_ad, xb[...].reshape(2 * half_rows, depth), 1, 0)
        sw_low.wait_recv()
        gb_out[0] = dot(
            s["low_own"][...], scot[pl.ds(half * blocks, blocks)].reshape(half_rows, width), 1, 0
        ) + dot(
            s["low_oth"][...], scot[pl.ds((1 - half) * blocks, blocks)].reshape(half_rows, width), 1, 0
        )

        gm_out[...] = gm3() / s["norms"][...]

        @pl.when(sec < 2)
        def _():
            ld_infl.wait()

        @pl.when(sec >= 2)
        def _():
            sw_car.wait_recv()

        val = term(0)
        for i, d in ways:
            val = val + landed(("d", d), 6 + i) + landed(("c", d), 4 + i)
        val = infl[...].astype(f32) + val * s["scale"][...]
        so_out[0] = val.astype(bf16)

        for copy in sw_hg:
            copy.wait_recv()
        hg_out[0] = (s["hg_own"][...] + s["hg_recv"][...].astype(f32)).astype(bf16)

        for copy in sent:
            copy.wait_send()

        @pl.when(sec >= 2)
        def _():
            for copy in sw_ret:
                copy.wait_send()

        @pl.when(sec < secs - 2)
        def _():
            sw_car.wait_send()


    return kernel


def hand_over(*refs):
    sems = refs[10]
    copies = [pltpu.make_async_copy(refs[i], refs[5 + i], sems.at[i]) for i in range(5)]
    for copy in copies:
        copy.start()
    for copy in copies:
        copy.wait()


def local(secs, tens, *args):
    (frozen, adapter_a, adapter_b, magnitude, hidden_fwd, carried, embedded, hidden_bwd, returned, head) = args
    depth, width = frozen.shape[1:]
    half_rows = hidden_fwd.shape[1]
    rings = tens // 2
    n_sems = 320
    shapes = {
        "w": pltpu.VMEM((depth, width), bf16),
        "a_own": pltpu.VMEM((8, depth), bf16),
        "a_oth": pltpu.VMEM((8, depth), bf16),
        "at": pltpu.VMEM((depth, 16), bf16),
        "b": pltpu.VMEM((16, width), bf16),
        "mag": pltpu.VMEM((1, width), f32),
        "norms": pltpu.VMEM((1, width), f32),
        "scale": pltpu.VMEM((1, width), f32),
        "xf": pltpu.VMEM((2, rings, 16, depth), bf16),
        "xb": pltpu.VMEM((2, half_rows, depth), bf16),
        "infl": pltpu.VMEM((16, width), bf16),
        "cot": pltpu.VMEM((tens, 16, width), bf16),
        "scot": pltpu.VMEM((tens, 16, width), bf16),
        "sq": pltpu.VMEM((1, width), f32),
        "sq_sib": pltpu.VMEM((1, width), f32),
        "sq_slots": pltpu.VMEM((rings, 1, width), f32),
        "gmp": pltpu.VMEM((1, width), f32),
        "gm_sib": pltpu.VMEM((1, width), f32),
        "gm_slots": pltpu.VMEM((rings, 1, width), f32),
        "lo": pltpu.VMEM((16, half_rows), f32),
        "lo_sib": pltpu.VMEM((16, half_rows), f32),
        "lo_slots": pltpu.VMEM((rings, 16, half_rows), f32),
        "low_own": pltpu.VMEM((16, half_rows), bf16),
        "low_oth": pltpu.VMEM((16, half_rows), bf16),
        "p_send": pltpu.VMEM((rings, 16, width), bf16),
        "p_recv": pltpu.VMEM((rings, 16, width), bf16),
        "pm": pltpu.VMEM((rings, 16, width), f32),
        "rs_send": pltpu.VMEM((8, 16, width), bf16),
        "rs_recv": pltpu.VMEM((8, 16, width), bf16),
        "rec": pltpu.VMEM((2 * half_rows, width), f32),
        "hg_send": pltpu.VMEM((half_rows, depth), bf16),
        "hg_recv": pltpu.VMEM((half_rows, depth), bf16),
        "hg_own": pltpu.VMEM((half_rows, depth), f32),
        "ad": pltpu.VMEM((2, 8, 2 * half_rows), f32),
        "ad_recv": pltpu.VMEM((8, 2 * half_rows), f32),
        "sems": pltpu.SemaphoreType.DMA((n_sems,)),
    }
    anywhere = pl.BlockSpec(memory_space=pl.ANY)
    results = pl.pallas_call(
        make_kernel(secs, tens, list(shapes), n_sems),
        out_shape=(
            pltpu.VMEM((1, 16, width), bf16),
            pltpu.VMEM((1, width), f32),
            pltpu.VMEM((1, 8, depth), f32),
            pltpu.VMEM((1, 16, width), f32),
            pltpu.VMEM((1, half_rows, depth), bf16),
        ),
        in_specs=[anywhere] * 10,
        out_specs=(pl.BlockSpec(memory_space=pltpu.VMEM),) * 5,
        scratch_shapes=list(shapes.values()),
        compiler_params=pltpu.CompilerParams(
            collective_id=0, has_side_effects=True, vmem_limit_bytes=62 * 1024 * 1024
        ),
    )(
        frozen,
        adapter_a,
        adapter_b,
        magnitude,
        hidden_fwd.reshape(half_rows // 32, 2, 16, depth),
        carried,
        embedded,
        hidden_bwd,
        returned,
        head,
    )
    return pl.pallas_call(
        hand_over,
        out_shape=[jax.ShapeDtypeStruct(r.shape, r.dtype) for r in results],
        in_specs=[pl.BlockSpec(memory_space=pltpu.VMEM)] * 5,
        out_specs=[anywhere] * 5,
        scratch_shapes=[pltpu.SemaphoreType.DMA((5,))],
        compiler_params=pltpu.CompilerParams(vmem_limit_bytes=4 * 1024 * 1024),
    )(*results)


def solution(mesh):
    secs, tens = mesh.shape["section"], mesh.shape["tensor"]
    placed = (
        P("section", "tensor", None),
        P("section", None, "tensor"),
        P("section", None, None),
        P("section", None),
        P("section", None, "tensor"),
        P("section", "tensor", None),
        P("tensor", None),
        P("section", None, "tensor"),
        P("section", "tensor", None),
        P("tensor", None),
    )

    def run(*args):
        return local(secs, tens, *args)

    return jax.shard_map(
        run,
        mesh=mesh,
        in_specs=placed,
        out_specs=(
            P("section", "tensor", None),
            P("section", None),
            P("section", None, "tensor"),
            P("section", None, None),
            P("section", None, "tensor"),
        ),
        check_vma=False,
    )
```
